32 devices in a mesh: gx: 4 (over z), gy: 4 (over y, x), gz: 2 (over core).
Axes of the slice: x: 2, y: 2, z: 4, core: 2. Of those that a mesh axis runs over, the one named last changes fastest.
Arguments:
- tensor: float32 [512, 256, 256], P('gx', 'gy', 'gz'), may hold values from -60 to 60
- factor_a: float32 [512, 64], P(('gx', 'gy', 'gz')), may hold values from -6 to 6
- factor_b: float32 [256, 64], P(('gy', 'gx', 'gz')), may hold values from -6 to 6
- factor_c: float32 [256, 64], P(('gz', 'gx', 'gy')), may hold values from -6 to 6
Outputs:
- slope_a: float32 [512, 64], P(('gx', 'gy', 'gz'))
- slope_b: float32 [256, 64], P(('gy', 'gx', 'gz'))
- slope_c: float32 [256, 64], P(('gz', 'gx', 'gy'))
The draws below stay inside these ranges and needn't reach their ends.
All inputs are finite; a program needn't handle non-finite values.
Results may differ from the reference program's by a relative error of at most 0.0003.
Values sent between devices are 32-bit elements; how exact they have to be, the bound alone decides.
A program may use at most 64 MiB of HBM per device.

```python
import math
import jax
import jax.numpy as jnp
from jax import lax

R = 64
STEPS = 2
I = 512
J = 256
K = 256


def factor_pair(key, row_count, salt):
    folded = jax.random.fold_in(key, salt)
    key_one, key_two, key_three, key_four = jax.random.split(folded, 4)
    row_scale = jnp.exp(jax.random.uniform(key_one, (row_count, 1), jnp.float32, math.log(0.4), math.log(4.0)))
    entries = jax.random.normal(key_two, (row_count, R), jnp.float32)
    common = 0.6 * jax.random.normal(key_three, (row_count, 1), jnp.float32)
    jitter = jax.random.normal(key_four, (row_count, R), jnp.float32)
    target = jnp.clip(0.5 * row_scale * (entries + common), -6.0, 6.0)
    initial = jnp.clip(target + 0.15 * row_scale * jitter, -6.0, 6.0)
    return (target, initial)


def draw_tensor(key, part):
    model_a = factor_pair(key, I, 1)[0]
    model_b = factor_pair(key, J, 2)[0]
    model_c = factor_pair(key, K, 3)[0]
    paired = (model_a[:, None, :] * model_b[None, :, :]).reshape(I * J, R)
    model = jnp.dot(paired, model_c.T, precision=lax.Precision.HIGHEST).reshape(I, J, K)
    extra_key = jax.random.fold_in(key, 4)
    extra = jax.random.normal(extra_key, (I, J, K), jnp.float32)
    return jnp.clip(model + 0.05 * extra, -60.0, 60.0)


def draw_factor_a(key, part):
    return factor_pair(key, I, 1)[1]


def draw_factor_b(key, part):
    return factor_pair(key, J, 2)[1]


def draw_factor_c(key, part):
    return factor_pair(key, K, 3)[1]


def setup_inputs(seed: int = 0) -> dict:
    splits = jax.random.split(jax.random.key(seed), 5)
    return {
        "tensor": draw_tensor(jax.random.fold_in(splits[4], 71), 0),
        "factor_a": draw_factor_a(jax.random.fold_in(splits[4], 71), 0),
        "factor_b": draw_factor_b(jax.random.fold_in(splits[4], 71), 0),
        "factor_c": draw_factor_c(jax.random.fold_in(splits[4], 71), 0),
    }


def reference(tensor, factor_a, factor_b, factor_c):
    highest = lax.Precision.HIGHEST
    step_size = 0.1
    first, second, third = factor_a, factor_b, factor_c
    for round_index in range(STEPS):
        gram_a = jnp.dot(first.T, first, precision=highest, preferred_element_type=jnp.float32)
        gram_b = jnp.dot(second.T, second, precision=highest, preferred_element_type=jnp.float32)
        gram_c = jnp.dot(third.T, third, precision=highest, preferred_element_type=jnp.float32)
        along_k = jnp.einsum("ijk,kr->ijr", tensor, third, precision=highest)
        moment_a = jnp.einsum("ijr,jr->ir", along_k, second, precision=highest)
        moment_b = jnp.einsum("ijr,ir->jr", along_k, first, precision=highest)
        along_i = jnp.einsum("ijk,ir->jkr", tensor, first, precision=highest)
        moment_c = jnp.einsum("jkr,jr->kr", along_i, second, precision=highest)
        slope_a = (jnp.dot(first, gram_b * gram_c, precision=highest) - moment_a) / (J * K)
        slope_b = (jnp.dot(second, gram_a * gram_c, precision=highest) - moment_b) / (I * K)
        slope_c = (jnp.dot(third, gram_a * gram_b, precision=highest) - moment_c) / (I * J)
        if round_index + 1 < STEPS:
            first = first - step_size * slope_a
            second = second - step_size * slope_b
            third = third - step_size * slope_c
    return slope_a, slope_b, slope_c
```

```python
import functools

import jax
import jax.numpy as jnp
from jax import lax
from jax.experimental import pallas as pl
from jax.experimental.pallas import tpu as pltpu
from jax.sharding import PartitionSpec as P

STEPS = 2
step_size = 0.1
HIGHEST = lax.Precision.HIGHEST
MESH = pl.DeviceIdType.MESH
CHUNK = 8


def twice(x):
    return jnp.concatenate([x, x], axis=1)


def left_half(shape):
    return lax.broadcasted_iota(jnp.int32, shape, 1) < shape[1] // 2


def split(x):
    high = x.astype(jnp.bfloat16).astype(jnp.float32)
    return high, x - high


def kernel(
    sizes,
    counts,
    tensor_hbm,
    own_a_ref,
    own_b_ref,
    own_c_ref,
    out_a_ref,
    out_b_ref,
    out_c_ref,
    tensor_ref,
    pair_ref,
    gat_a,
    gat_b,
    gat_c,
    blk_a,
    blk_b,
    blk_c,
    sum_a,
    sum_b,
    sum_c,
    push_a,
    push_b,
    push_c,
    pull_a,
    pull_b,
    pull_c,
    gram_a,
    gram_b,
    gram_c,
    load_sem,
    send_sem,
    recv_sem,
):
    nx, ny, nz = sizes
    gx, gy, gz = (lax.axis_index(name) for name in ("gx", "gy", "gz"))
    rank = own_a_ref.shape[1]
    wide = 2 * rank
    n_i, n_j, n_k = tensor_ref.shape
    n_chunks = n_i // CHUNK

    pieces = load_sem.shape[0]
    piece = n_i // pieces
    loads = [
        pltpu.make_async_copy(
            tensor_hbm.at[pl.ds(p * piece, piece)],
            tensor_ref.at[pl.ds(p * piece, piece)],
            load_sem.at[p],
        )
        for p in range(pieces)
    ]
    for load in loads:
        load.start()

    xs = [lax.rem(gx + d, nx) for d in range(nx)]
    ys = [lax.rem(gy + d, ny) for d in range(ny)]
    zs = [lax.rem(gz + d, nz) for d in range(nz)]

    def at(dx, dy, dz):
        return {"gx": xs[dx], "gy": ys[dy], "gz": zs[dz]}

    greeted = [
        (dx, dy, dz)
        for dx in range(nx)
        for dy in range(ny)
        for dz in range(nz)
        if 0 in (dx, dy, dz) and (dx or dy or dz)
    ]
    barrier = pltpu.get_barrier_semaphore()
    for offset in greeted:
        pl.semaphore_signal(barrier, inc=1, device_id=at(*offset), device_id_type=MESH)

    peers_a = [
        (at(0, dy, dz), ys[dy] * nz + zs[dz]) for dy in range(ny) for dz in range(nz) if dy or dz
    ]
    peers_b = [
        (at(dx, 0, dz), xs[dx] * nz + zs[dz]) for dx in range(nx) for dz in range(nz) if dx or dz
    ]
    peers_c = [
        (at(dx, dy, 0), xs[dx] * ny + ys[dy]) for dx in range(nx) for dy in range(ny) if dx or dy
    ]
    groups = (
        (peers_a, gy * nz + gz, 0),
        (peers_b, gx * nz + gz, 1),
        (peers_c, gx * ny + gy, 2),
    )
    lines = (
        ([(at(d, 0, 0), xs[d]) for d in range(1, nx)], gx, 0),
        ([(at(0, d, 0), ys[d]) for d in range(1, ny)], gy, 1),
        ([(at(0, 0, d), zs[d]) for d in range(1, nz)], gz, 2),
    )

    def transfer(src, dst, slot, device):
        return pltpu.make_async_remote_copy(
            src_ref=src,
            dst_ref=dst,
            send_sem=send_sem.at[slot],
            recv_sem=recv_sem.at[slot],
            device_id=device,
            device_id_type=MESH,
        )

    def all_of(buffer, peers, slot):
        some = buffer.at[pl.ds(0, len(peers))]
        return transfer(some, some, slot, peers[0][0])

    finals = []

    def gather(buffers, round_index, values):
        for (peers, me, which), buffer, value in zip(groups, buffers, values):
            slot = 9 * round_index + which
            buffer[round_index, me] = value
            for device, _ in peers:
                mine = buffer.at[round_index, me]
                transfer(mine, mine, slot, device).start()
            finals.append((buffer.at[round_index], peers, slot))

    gathers = (gat_a, gat_b, gat_c)
    own = [twice(ref[...]) for ref in (own_a_ref, own_b_ref, own_c_ref)]
    pl.semaphore_wait(barrier, len(greeted))
    gather(gathers, 0, own)

    for p, load in enumerate(loads):
        load.wait()

        def prepare(c, carry):
            block = tensor_ref[pl.ds(c * CHUNK, CHUNK)].reshape(CHUNK * n_j, n_k)
            high, low = split(block)
            rows = pl.ds(pl.multiple_of(c * (CHUNK * n_j), CHUNK * n_j), CHUNK * n_j)
            pair_ref[rows, pl.ds(0, n_k)] = high.astype(jnp.bfloat16)
            pair_ref[rows, pl.ds(n_k, n_k)] = low.astype(jnp.bfloat16)
            return carry

        lax.fori_loop(p * piece // CHUNK, (p + 1) * piece // CHUNK, prepare, 0)

    for round_index in range(STEPS):
        for (peers, me, which), buffer, block in zip(groups, gathers, (blk_a, blk_b, blk_c)):
            all_of(buffer.at[round_index], peers, 9 * round_index + which).wait_recv()
            rows = buffer.shape[2]
            for p in range(len(peers) + 1):
                block[p * rows : (p + 1) * rows] = buffer[round_index, p]

        half = rank // 2
        grams = (gram_a, gram_b, gram_c)
        for (peers, me, which), block, gram in zip(lines, (blk_a, blk_b, blk_c), grams):
            slot = 9 * round_index + 3 + which
            matrix = block[...]
            full = jnp.dot(
                matrix.T[:rank], matrix, precision=HIGHEST, preferred_element_type=jnp.float32
            )
            packed = jnp.where(left_half((half, wide)), full[:half], full[half:])
            gram[round_index, me] = packed
            for device, _ in peers:
                mine = gram.at[round_index, me]
                transfer(mine, mine, slot, device).start()
            finals.append((gram.at[round_index], peers, slot))

        block_b = blk_b[...]
        high_c, low_c = split(blk_c[...])
        mixed_c = jnp.where(left_half((n_k, wide)), high_c, low_c).astype(jnp.bfloat16)
        weights = jnp.concatenate([mixed_c, mixed_c], axis=0)

        sum_b[...] = jnp.zeros_like(sum_b)
        sum_c[...] = jnp.zeros_like(sum_c)

        def contract(c, carry):
            rows = pl.ds(pl.multiple_of(c * (CHUNK * n_j), CHUNK * n_j), CHUNK * n_j)
            pair = pair_ref[rows, :]
            part_a = pl.ds(pl.multiple_of(c * CHUNK, CHUNK), CHUNK)
            rows_a = blk_a[part_a, :]
            along = jnp.dot(pair, weights, preferred_element_type=jnp.float32)
            along = along.reshape(CHUNK, n_j, wide)
            sum_a[part_a, :] = jnp.sum(along * block_b[None], axis=1)
            sum_b[...] += jnp.sum(along * rows_a[:, None, :], axis=0)
            paired = (rows_a[:, None, :] * block_b[None]).reshape(CHUNK * n_j, wide)
            high, low = split(paired)
            mixed = jnp.where(left_half(paired.shape), high, low).astype(jnp.bfloat16)
            sum_c[...] += lax.dot_general(
                mixed, pair, (((0,), (0,)), ((), ())), preferred_element_type=jnp.float32
            )
            return carry

        lax.fori_loop(0, n_chunks, contract, 0)

        moment_a = sum_a[...]
        moment_b = sum_b[...]
        flipped = sum_c[...]
        flipped = flipped[:, :n_k] + flipped[:, n_k:]
        flipped = flipped[:rank] + flipped[rank:]
        moments = (
            moment_a + pltpu.roll(moment_a, rank, 1),
            moment_b + pltpu.roll(moment_b, rank, 1),
            jnp.concatenate([flipped, flipped], axis=0).T,
        )
        pushes, pulls = (push_a, push_b, push_c), (pull_a, pull_b, pull_c)
        for (peers, me, which), moment, push, pull in zip(groups, moments, pushes, pulls):
            slot = 9 * round_index + 6 + which
            rows = push.shape[2]
            for p in range(len(peers) + 1):
                push[round_index, p] = moment[p * rows : (p + 1) * rows]
            for device, place in peers:
                transfer(
                    push.at[round_index, place], pull.at[round_index, me], slot, device
                ).start()
            pull[round_index, me] = push[round_index, me]
            finals.append((pull.at[round_index], peers, slot))

        totals = []
        for (peers, me, which), gram in zip(lines, grams):
            all_of(gram.at[round_index], peers, 9 * round_index + 3 + which).wait_recv()
            totals.append(sum(gram[round_index, p] for p in range(len(peers) + 1)))

        def unpack(packed):
            turned = pltpu.roll(packed, rank, 1)
            left = left_half(packed.shape)
            return jnp.concatenate(
                [jnp.where(left, packed, turned), jnp.where(left, turned, packed)], axis=0
            )

        products = (
            unpack(totals[1] * totals[2]),
            unpack(totals[0] * totals[2]),
            unpack(totals[0] * totals[1]),
        )
        heads = [
            jnp.dot(x[:, :rank], product, precision=HIGHEST, preferred_element_type=jnp.float32)
            for x, product in zip(own, products)
        ]
        slopes = []
        for (peers, me, which), pull, head, count in zip(groups, pulls, heads, counts):
            all_of(pull.at[round_index], peers, 9 * round_index + 6 + which).wait_recv()
            moment = sum(pull[round_index, p] for p in range(len(peers) + 1))
            slopes.append((head - moment) / count)
        if round_index + 1 < STEPS:
            own = [x - step_size * slope for x, slope in zip(own, slopes)]
            gather(gathers, round_index + 1, own)

    for ref, slope in zip((out_a_ref, out_b_ref, out_c_ref), slopes):
        ref[...] = slope[:, :rank]
    for buffer, peers, slot in finals:
        all_of(buffer, peers, slot).wait_send()


def shards(sizes, tensor, factor_a, factor_b, factor_c):
    nx, ny, nz = sizes
    n_i, n_j, n_k = tensor.shape
    rank = factor_a.shape[1]
    wide = 2 * rank
    all_i, all_j, all_k = float(n_i * nx), float(n_j * ny), float(n_k * nz)
    counts = (all_j * all_k, all_i * all_k, all_i * all_j)
    f32 = jnp.float32
    rows = [x.shape[0] for x in (factor_a, factor_b, factor_c)]
    sides = [ny * nz, nx * nz, nx * ny]
    slots = [pltpu.VMEM((STEPS, n, r, wide), f32) for n, r in zip(sides, rows)]
    blocks = [pltpu.VMEM((n, wide), f32) for n in (n_i, n_j, n_k)]
    return pl.pallas_call(
        functools.partial(kernel, sizes, counts),
        out_shape=[jax.ShapeDtypeStruct(x.shape, f32) for x in (factor_a, factor_b, factor_c)],
        in_specs=[pl.BlockSpec(memory_space=pl.ANY)] + [pl.BlockSpec(memory_space=pltpu.VMEM)] * 3,
        out_specs=[pl.BlockSpec(memory_space=pltpu.VMEM)] * 3,
        scratch_shapes=[
            pltpu.VMEM(tensor.shape, f32),
            pltpu.VMEM((n_i * n_j, 2 * n_k), jnp.bfloat16),
            *slots,
            *blocks,
            pltpu.VMEM((n_i, wide), f32),
            pltpu.VMEM((n_j, wide), f32),
            pltpu.VMEM((wide, 2 * n_k), f32),
            *slots,
            *slots,
            *[pltpu.VMEM((STEPS, n, rank // 2, wide), f32) for n in sizes],
            pltpu.SemaphoreType.DMA((4,)),
            pltpu.SemaphoreType.DMA((9 * STEPS,)),
            pltpu.SemaphoreType.DMA((9 * STEPS,)),
        ],
        compiler_params=pltpu.CompilerParams(
            collective_id=0, has_side_effects=True, vmem_limit_bytes=48 * 1024 * 1024
        ),
    )(tensor, factor_a, factor_b, factor_c)


def solution(mesh):
    sizes = tuple(mesh.shape[name] for name in ("gx", "gy", "gz"))
    rows = (
        P(("gx", "gy", "gz"), None),
        P(("gy", "gx", "gz"), None),
        P(("gz", "gx", "gy"), None),
    )
    return jax.shard_map(
        functools.partial(shards, sizes),
        mesh=mesh,
        in_specs=(P("gx", "gy", "gz"), *rows),
        out_specs=rows,
        check_vma=False,
    )
```

```python
import functools

import jax
import jax.numpy as jnp
from jax import lax
from jax.experimental import pallas as pl
from jax.experimental.pallas import tpu as pltpu
from jax.sharding import PartitionSpec as P

STEPS = 2
step_size = 0.1
HIGHEST = lax.Precision.HIGHEST
MESH = pl.DeviceIdType.MESH
CHUNK = 8
CHUNK_C = 16


def twice(x):
    return jnp.concatenate([x, x], axis=1)


def left_half(shape):
    return lax.broadcasted_iota(jnp.int32, shape, 1) < shape[1] // 2


def packed_rows(rows):
    return rows // 2 if rows % 2 == 0 else rows


def pack(x):
    rows = x.shape[0]
    if rows % 2:
        return x
    return jnp.where(left_half((rows // 2, x.shape[1])), x[: rows // 2], x[rows // 2 :])


def unpack(x, rows):
    if rows % 2:
        return (x,)
    turned = pltpu.roll(x, x.shape[1] // 2, 1)
    left = left_half(x.shape)
    return (jnp.where(left, x, turned), jnp.where(left, turned, x))


def split(x):
    high = x.astype(jnp.bfloat16).astype(jnp.float32)
    return high, x - high


def kernel(
    sizes,
    counts,
    tensor_hbm,
    own_a_hbm,
    own_b_hbm,
    own_c_hbm,
    out_a_ref,
    out_b_ref,
    out_c_ref,
    own_a_ref,
    own_b_ref,
    own_c_ref,
    tensor_ref,
    pair_ref,
    gat_a,
    gat_b,
    gat_c,
    blk_a,
    blk_b,
    blk_c,
    sum_a,
    sum_b,
    sum_c,
    push_a,
    push_b,
    push_c,
    pull_a,
    pull_b,
    pull_c,
    gram_a,
    gram_b,
    gram_c,
    own_sem,
    load_sem,
    send_sem,
    recv_sem,
):
    nx, ny, nz = sizes
    gx, gy, gz = (lax.axis_index(name) for name in ("gx", "gy", "gz"))
    rank = own_a_ref.shape[1]
    wide = 2 * rank
    n_i, n_j, n_k = tensor_ref.shape

    owned = (own_a_ref, own_b_ref, own_c_ref)
    own_loads = [
        pltpu.make_async_copy(hbm, ref, own_sem.at[p])
        for p, (hbm, ref) in enumerate(zip((own_a_hbm, own_b_hbm, own_c_hbm), owned))
    ]
    for load in own_loads:
        load.start()

    pieces = load_sem.shape[0]
    piece = n_i // pieces
    loads = [
        pltpu.make_async_copy(
            tensor_hbm.at[pl.ds(p * piece, piece)],
            tensor_ref.at[pl.ds(p * piece, piece)],
            load_sem.at[p],
        )
        for p in range(pieces)
    ]
    for load in loads:
        load.start()

    xs = [lax.rem(gx + d, nx) for d in range(nx)]
    ys = [lax.rem(gy + d, ny) for d in range(ny)]
    zs = [lax.rem(gz + d, nz) for d in range(nz)]

    def at(dx, dy, dz):
        return {"gx": xs[dx], "gy": ys[dy], "gz": zs[dz]}

    greeted = [
        (dx, dy, dz)
        for dx in range(nx)
        for dy in range(ny)
        for dz in range(nz)
        if 0 in (dx, dy, dz) and (dx or dy or dz)
    ]
    barrier = pltpu.get_barrier_semaphore()
    for offset in greeted:
        pl.semaphore_signal(barrier, inc=1, device_id=at(*offset), device_id_type=MESH)

    peers_a = [
        (at(0, dy, dz), ys[dy] * nz + zs[dz]) for dy in range(ny) for dz in range(nz) if dy or dz
    ]
    peers_b = [
        (at(dx, 0, dz), xs[dx] * nz + zs[dz]) for dx in range(nx) for dz in range(nz) if dx or dz
    ]
    peers_c = [
        (at(dx, dy, 0), xs[dx] * ny + ys[dy]) for dx in range(nx) for dy in range(ny) if dx or dy
    ]
    groups = (
        (peers_a, gy * nz + gz, 0),
        (peers_b, gx * nz + gz, 1),
        (peers_c, gx * ny + gy, 2),
    )
    lines = (
        ([(at(d, 0, 0), xs[d]) for d in range(1, nx)], gx, 0),
        ([(at(0, d, 0), ys[d]) for d in range(1, ny)], gy, 1),
        ([(at(0, 0, d), zs[d]) for d in range(1, nz)], gz, 2),
    )

    def transfer(src, dst, slot, device):
        return pltpu.make_async_remote_copy(
            src_ref=src,
            dst_ref=dst,
            send_sem=send_sem.at[slot],
            recv_sem=recv_sem.at[slot],
            device_id=device,
            device_id_type=MESH,
        )

    def all_of(buffer, peers, slot):
        some = buffer.at[pl.ds(0, len(peers))]
        return transfer(some, some, slot, peers[0][0])

    finals = []

    def gather(buffers, round_index, values):
        for (peers, me, which), buffer, value in zip(groups, buffers, values):
            slot = 9 * round_index + which
            buffer[round_index, me] = pack(value)
            for device, _ in peers:
                mine = buffer.at[round_index, me]
                transfer(mine, mine, slot, device).start()
            finals.append((buffer.at[round_index], peers, slot))

    gathers = (gat_a, gat_b, gat_c)
    for load in own_loads:
        load.wait()
    own = [twice(ref[...]) for ref in owned]
    pl.semaphore_wait(barrier, len(greeted))
    gather(gathers, 0, own)

    for p, load in enumerate(loads):
        load.wait()

        def prepare(c, carry):
            block = tensor_ref[pl.ds(c * CHUNK, CHUNK)].reshape(CHUNK * n_j, n_k)
            high, low = split(block)
            rows = pl.ds(pl.multiple_of(c * (CHUNK * n_j), CHUNK * n_j), CHUNK * n_j)
            pair_ref[rows, pl.ds(0, n_k)] = high.astype(jnp.bfloat16)
            pair_ref[rows, pl.ds(n_k, n_k)] = low.astype(jnp.bfloat16)
            return carry

        lax.fori_loop(p * piece // CHUNK, (p + 1) * piece // CHUNK, prepare, 0)

    blocks = (blk_a, blk_b, blk_c)
    grams = (gram_a, gram_b, gram_c)
    pushes, pulls = (push_a, push_b, push_c), (pull_a, pull_b, pull_c)
    half = rank // 2

    def receive(round_index, which):
        peers, me, _ = groups[which]
        buffer, block = gathers[which], blocks[which]
        all_of(buffer.at[round_index], peers, 9 * round_index + which).wait_recv()
        rows = owned[which].shape[0]
        for p in range(len(peers) + 1):
            parts = unpack(buffer[round_index, p], rows)
            step = rows // len(parts)
            for q, part in enumerate(parts):
                block[p * rows + q * step : p * rows + (q + 1) * step] = part

    def send_gram(round_index, which):
        peers, me, _ = lines[which]
        gram, slot = grams[which], 9 * round_index + 3 + which
        matrix = blocks[which][...]
        full = jnp.dot(
            matrix.T[:rank], matrix, precision=HIGHEST, preferred_element_type=jnp.float32
        )
        gram[round_index, me] = pack(full)
        for device, _ in peers:
            mine = gram.at[round_index, me]
            transfer(mine, mine, slot, device).start()
        finals.append((gram.at[round_index], peers, slot))

    def scatter(round_index, which, moment):
        peers, me, _ = groups[which]
        push, pull, slot = pushes[which], pulls[which], 9 * round_index + 6 + which
        rows = owned[which].shape[0]
        for p in range(len(peers) + 1):
            push[round_index, p] = pack(moment[p * rows : (p + 1) * rows])
        for device, place in peers:
            transfer(push.at[round_index, place], pull.at[round_index, me], slot, device).start()
        pull[round_index, me] = push[round_index, me]
        finals.append((pull.at[round_index], peers, slot))

    for round_index in range(STEPS):
        receive(round_index, 0)
        receive(round_index, 1)
        send_gram(round_index, 0)
        send_gram(round_index, 1)
        block_b = blk_b[...]

        sum_c[...] = jnp.zeros_like(sum_c)

        def contract_c(c, carry):
            rows = pl.ds(pl.multiple_of(c * (CHUNK_C * n_j), CHUNK_C * n_j), CHUNK_C * n_j)
            rows_a = blk_a[pl.ds(pl.multiple_of(c * CHUNK_C, CHUNK_C), CHUNK_C), :]
            paired = (rows_a[:, None, :] * block_b[None]).reshape(CHUNK_C * n_j, wide)
            high, low = split(paired)
            mixed = jnp.where(left_half(paired.shape), high, low).astype(jnp.bfloat16)
            sum_c[...] += lax.dot_general(
                mixed,
                pair_ref[rows, :],
                (((0,), (0,)), ((), ())),
                preferred_element_type=jnp.float32,
            )
            return carry

        lax.fori_loop(0, n_i // CHUNK_C, contract_c, 0, unroll=2)
        flipped = sum_c[...]
        flipped = flipped[:, :n_k] + flipped[:, n_k:]
        flipped = flipped[:rank] + flipped[rank:]
        scatter(round_index, 2, jnp.concatenate([flipped, flipped], axis=0).T)

        receive(round_index, 2)
        send_gram(round_index, 2)
        high_c, low_c = split(blk_c[...])
        mixed_c = jnp.where(left_half((n_k, wide)), high_c, low_c).astype(jnp.bfloat16)
        weights = jnp.concatenate([mixed_c, mixed_c], axis=0)
        sum_b[...] = jnp.zeros_like(sum_b)

        def contract_ab(c, carry):
            rows = pl.ds(pl.multiple_of(c * (CHUNK * n_j), CHUNK * n_j), CHUNK * n_j)
            part_a = pl.ds(pl.multiple_of(c * CHUNK, CHUNK), CHUNK)
            rows_a = blk_a[part_a, :]
            along = jnp.dot(pair_ref[rows, :], weights, preferred_element_type=jnp.float32)
            along = along.reshape(CHUNK, n_j, wide)
            sum_a[part_a, :] = jnp.sum(along * block_b[None], axis=1)
            sum_b[...] += jnp.sum(along * rows_a[:, None, :], axis=0)
            return carry

        lax.fori_loop(0, n_i // CHUNK, contract_ab, 0, unroll=4)
        moment_a, moment_b = sum_a[...], sum_b[...]
        scatter(round_index, 0, moment_a + pltpu.roll(moment_a, rank, 1))
        scatter(round_index, 1, moment_b + pltpu.roll(moment_b, rank, 1))

        totals = []
        for (peers, me, which), gram in zip(lines, grams):
            all_of(gram.at[round_index], peers, 9 * round_index + 3 + which).wait_recv()
            totals.append(sum(gram[round_index, p] for p in range(len(peers) + 1)))
        products = [
            jnp.concatenate(unpack(totals[p] * totals[q], rank), axis=0)
            for p, q in ((1, 2), (0, 2), (0, 1))
        ]
        heads = [
            jnp.dot(x[:, :rank], product, precision=HIGHEST, preferred_element_type=jnp.float32)
            for x, product in zip(own, products)
        ]
        slopes = [None] * 3
        for which in (2, 0, 1):
            peers = groups[which][0]
            pull, rows = pulls[which], owned[which].shape[0]
            all_of(pull.at[round_index], peers, 9 * round_index + 6 + which).wait_recv()
            moment = sum(pull[round_index, p] for p in range(len(peers) + 1))
            moment = jnp.concatenate(unpack(moment, rows), axis=0)
            slopes[which] = (heads[which] - moment) / counts[which]
        if round_index + 1 < STEPS:
            own = [x - step_size * slope for x, slope in zip(own, slopes)]
            gather(gathers, round_index + 1, own)

    for ref, slope in zip((out_a_ref, out_b_ref, out_c_ref), slopes):
        ref[...] = slope[:, :rank]
    for buffer, peers, slot in finals:
        all_of(buffer, peers, slot).wait_send()


def store(from_a, from_b, from_c, to_a, to_b, to_c, sem):
    copies = [
        pltpu.make_async_copy(source, target, sem.at[p])
        for p, (source, target) in enumerate(((from_a, to_a), (from_b, to_b), (from_c, to_c)))
    ]
    for copy in copies:
        copy.start()
    for copy in copies:
        copy.wait()


def shards(sizes, tensor, factor_a, factor_b, factor_c):
    nx, ny, nz = sizes
    n_i, n_j, n_k = tensor.shape
    rank = factor_a.shape[1]
    wide = 2 * rank
    all_i, all_j, all_k = float(n_i * nx), float(n_j * ny), float(n_k * nz)
    counts = (all_j * all_k, all_i * all_k, all_i * all_j)
    f32 = jnp.float32
    rows = [x.shape[0] for x in (factor_a, factor_b, factor_c)]
    sides = [ny * nz, nx * nz, nx * ny]
    slots = [pltpu.VMEM((STEPS, n, packed_rows(r), wide), f32) for n, r in zip(sides, rows)]
    blocks = [pltpu.VMEM((n, wide), f32) for n in (n_i, n_j, n_k)]
    slopes = pl.pallas_call(
        functools.partial(kernel, sizes, counts),
        out_shape=[jax.ShapeDtypeStruct(x.shape, f32) for x in (factor_a, factor_b, factor_c)],
        in_specs=[pl.BlockSpec(memory_space=pltpu.HBM)] * 4,
        out_specs=[pl.BlockSpec(memory_space=pltpu.VMEM)] * 3,
        scratch_shapes=[
            *[pltpu.VMEM(x.shape, f32) for x in (factor_a, factor_b, factor_c)],
            pltpu.VMEM(tensor.shape, f32),
            pltpu.VMEM((n_i * n_j, 2 * n_k), jnp.bfloat16),
            *slots,
            *blocks,
            pltpu.VMEM((n_i, wide), f32),
            pltpu.VMEM((n_j, wide), f32),
            pltpu.VMEM((wide, 2 * n_k), f32),
            *slots,
            *slots,
            *[pltpu.VMEM((STEPS, n, rank // 2, wide), f32) for n in sizes],
            pltpu.SemaphoreType.DMA((3,)),
            pltpu.SemaphoreType.DMA((4,)),
            pltpu.SemaphoreType.DMA((9 * STEPS,)),
            pltpu.SemaphoreType.DMA((9 * STEPS,)),
        ],
        compiler_params=pltpu.CompilerParams(
            collective_id=0, has_side_effects=True, vmem_limit_bytes=60 * 1024 * 1024
        ),
    )(tensor, factor_a, factor_b, factor_c)
    return pl.pallas_call(
        store,
        out_shape=[jax.ShapeDtypeStruct(x.shape, f32) for x in (factor_a, factor_b, factor_c)],
        in_specs=[pl.BlockSpec(memory_space=pl.ANY)] * 3,
        out_specs=[pl.BlockSpec(memory_space=pltpu.HBM)] * 3,
        scratch_shapes=[pltpu.SemaphoreType.DMA((3,))],
        compiler_params=pltpu.CompilerParams(vmem_limit_bytes=60 * 1024 * 1024),
    )(*slopes)


def solution(mesh):
    sizes = tuple(mesh.shape[name] for name in ("gx", "gy", "gz"))
    rows = (
        P(("gx", "gy", "gz"), None),
        P(("gy", "gx", "gz"), None),
        P(("gz", "gx", "gy"), None),
    )
    return jax.shard_map(
        functools.partial(shards, sizes),
        mesh=mesh,
        in_specs=(P("gx", "gy", "gz"), *rows),
        out_specs=rows,
        check_vma=False,
    )
```

```python
import functools

import jax
import jax.numpy as jnp
from jax import lax
from jax.experimental import pallas as pl
from jax.experimental.pallas import tpu as pltpu
from jax.sharding import PartitionSpec as P

STEPS = 2
step_size = 0.1
MESH = pl.DeviceIdType.MESH
CHUNK = 8
CHUNK_C = 16


def twice(x):
    return jnp.concatenate([x, x], axis=1)


def left_half(shape):
    return lax.broadcasted_iota(jnp.int32, shape, 1) < shape[1] // 2


def packed_rows(rows):
    return rows // 2 if rows % 2 == 0 else rows


def pack(x):
    rows = x.shape[0]
    if rows % 2:
        return x
    return jnp.where(left_half((rows // 2, x.shape[1])), x[: rows // 2], x[rows // 2 :])


def unpack(x, rows):
    if rows % 2:
        return (x,)
    turned = pltpu.roll(x, x.shape[1] // 2, 1)
    left = left_half(x.shape)
    return (jnp.where(left, x, turned), jnp.where(left, turned, x))


def split(x):
    high = x.astype(jnp.bfloat16).astype(jnp.float32)
    return high, x - high


def mix(x):
    high, low = split(x)
    return jnp.where(left_half(x.shape), high, low).astype(jnp.bfloat16)


def kernel(
    sizes,
    counts,
    tensor_hbm,
    own_a_hbm,
    own_b_hbm,
    own_c_hbm,
    out_a_ref,
    out_b_ref,
    out_c_ref,
    own_a_ref,
    own_b_ref,
    own_c_ref,
    tensor_ref,
    pair_ref,
    gat_a,
    gat_b,
    gat_c,
    blk_a,
    blk_b,
    blk_c,
    sum_a,
    sum_b,
    sum_c,
    push_a,
    push_b,
    push_c,
    pull_a,
    pull_b,
    pull_c,
    gram_a,
    gram_b,
    gram_c,
    own_sem,
    load_sem,
    send_sem,
    recv_sem,
):
    nx, ny, nz = sizes
    gx, gy, gz = (lax.axis_index(name) for name in ("gx", "gy", "gz"))
    rank = own_a_ref.shape[1]
    wide = 2 * rank
    n_i, n_j, n_k = tensor_ref.shape

    owned = (own_a_ref, own_b_ref, own_c_ref)
    own_loads = [
        pltpu.make_async_copy(hbm, ref, own_sem.at[p])
        for p, (hbm, ref) in enumerate(zip((own_a_hbm, own_b_hbm, own_c_hbm), owned))
    ]
    for load in own_loads:
        load.start()

    pieces = load_sem.shape[0]
    piece = n_i // pieces
    loads = [
        pltpu.make_async_copy(
            tensor_hbm.at[pl.ds(p * piece, piece)],
            tensor_ref.at[pl.ds(p * piece, piece)],
            load_sem.at[p],
        )
        for p in range(pieces)
    ]
    for load in loads:
        load.start()

    xs = [lax.rem(gx + d, nx) for d in range(nx)]
    ys = [lax.rem(gy + d, ny) for d in range(ny)]
    zs = [lax.rem(gz + d, nz) for d in range(nz)]

    def at(dx, dy, dz):
        return {"gx": xs[dx], "gy": ys[dy], "gz": zs[dz]}

    greeted = [
        (dx, dy, dz)
        for dx in range(nx)
        for dy in range(ny)
        for dz in range(nz)
        if 0 in (dx, dy, dz) and (dx or dy or dz)
    ]
    barrier = pltpu.get_barrier_semaphore()
    for offset in greeted:
        pl.semaphore_signal(barrier, inc=1, device_id=at(*offset), device_id_type=MESH)

    peers_a = [
        (at(0, dy, dz), ys[dy] * nz + zs[dz]) for dy in range(ny) for dz in range(nz) if dy or dz
    ]
    peers_b = [
        (at(dx, 0, dz), xs[dx] * nz + zs[dz]) for dx in range(nx) for dz in range(nz) if dx or dz
    ]
    peers_c = [
        (at(dx, dy, 0), xs[dx] * ny + ys[dy]) for dx in range(nx) for dy in range(ny) if dx or dy
    ]
    groups = (
        (peers_a, gy * nz + gz, 0),
        (peers_b, gx * nz + gz, 1),
        (peers_c, gx * ny + gy, 2),
    )
    lines = (
        ([(at(d, 0, 0), xs[d]) for d in range(1, nx)], gx, 0),
        ([(at(0, d, 0), ys[d]) for d in range(1, ny)], gy, 1),
        ([(at(0, 0, d), zs[d]) for d in range(1, nz)], gz, 2),
    )

    def transfer(src, dst, slot, device):
        return pltpu.make_async_remote_copy(
            src_ref=src,
            dst_ref=dst,
            send_sem=send_sem.at[slot],
            recv_sem=recv_sem.at[slot],
            device_id=device,
            device_id_type=MESH,
        )

    def all_of(buffer, peers, slot):
        some = buffer.at[pl.ds(0, len(peers))]
        return transfer(some, some, slot, peers[0][0])

    finals = []

    gathers = (gat_a, gat_b, gat_c)

    def gather(round_index, which, value):
        peers, me, _ = groups[which]
        buffer, slot = gathers[which], 9 * round_index + which
        buffer[round_index, me] = pack(value)
        for device, _ in peers:
            mine = buffer.at[round_index, me]
            transfer(mine, mine, slot, device).start()
        finals.append((buffer.at[round_index], peers, slot))

    for load in own_loads:
        load.wait()
    own = [twice(ref[...]) for ref in owned]
    pl.semaphore_wait(barrier, len(greeted))
    for which in range(3):
        gather(0, which, own[which])

    for p, load in enumerate(loads):
        load.wait()

        def prepare(c, carry):
            block = tensor_ref[pl.ds(c * CHUNK, CHUNK)].reshape(CHUNK * n_j, n_k)
            high, low = split(block)
            rows = pl.ds(pl.multiple_of(c * (CHUNK * n_j), CHUNK * n_j), CHUNK * n_j)
            pair_ref[rows, pl.ds(0, n_k)] = high.astype(jnp.bfloat16)
            pair_ref[rows, pl.ds(n_k, n_k)] = low.astype(jnp.bfloat16)
            return carry

        lax.fori_loop(p * piece // CHUNK, (p + 1) * piece // CHUNK, prepare, 0)

    blocks = (blk_a, blk_b, blk_c)
    grams = (gram_a, gram_b, gram_c)
    pushes, pulls = (push_a, push_b, push_c), (pull_a, pull_b, pull_c)
    half = rank // 2

    def receive(round_index, which):
        peers, me, _ = groups[which]
        buffer, block = gathers[which], blocks[which]
        all_of(buffer.at[round_index], peers, 9 * round_index + which).wait_recv()
        rows = owned[which].shape[0]
        for p in range(len(peers) + 1):
            parts = unpack(buffer[round_index, p], rows)
            step = rows // len(parts)
            for q, part in enumerate(parts):
                block[p * rows + q * step : p * rows + (q + 1) * step] = part

    def send_gram(round_index, which):
        peers, me, _ = lines[which]
        gram, slot = grams[which], 9 * round_index + 3 + which
        mixed = mix(blocks[which][...])
        full = lax.dot_general(
            mixed, mixed, (((0,), (0,)), ((), ())), preferred_element_type=jnp.float32
        )
        full = full[:rank] + full[rank:]
        full = full + pltpu.roll(full, rank, 1)
        gram[round_index, me] = pack(full)
        for device, _ in peers:
            mine = gram.at[round_index, me]
            transfer(mine, mine, slot, device).start()
        finals.append((gram.at[round_index], peers, slot))

    def scatter(round_index, which, moment):
        peers, me, _ = groups[which]
        push, pull, slot = pushes[which], pulls[which], 9 * round_index + 6 + which
        rows = owned[which].shape[0]
        for p in range(len(peers) + 1):
            push[round_index, p] = pack(moment[p * rows : (p + 1) * rows])
        for device, place in peers:
            transfer(push.at[round_index, place], pull.at[round_index, me], slot, device).start()
        pull[round_index, me] = push[round_index, me]
        finals.append((pull.at[round_index], peers, slot))

    for round_index in range(STEPS):
        receive(round_index, 0)
        receive(round_index, 1)
        send_gram(round_index, 0)
        send_gram(round_index, 1)
        block_b = blk_b[...]

        sum_c[...] = jnp.zeros_like(sum_c)

        def contract_c(c, carry):
            rows = pl.ds(pl.multiple_of(c * (CHUNK_C * n_j), CHUNK_C * n_j), CHUNK_C * n_j)
            rows_a = blk_a[pl.ds(pl.multiple_of(c * CHUNK_C, CHUNK_C), CHUNK_C), :]
            paired = (rows_a[:, None, :] * block_b[None]).reshape(CHUNK_C * n_j, wide)
            mixed = mix(paired)
            sum_c[...] += lax.dot_general(
                mixed,
                pair_ref[rows, :],
                (((0,), (0,)), ((), ())),
                preferred_element_type=jnp.float32,
            )
            return carry

        lax.fori_loop(0, n_i // CHUNK_C, contract_c, 0, unroll=2)
        flipped = sum_c[...]
        flipped = flipped[:, :n_k] + flipped[:, n_k:]
        flipped = flipped[:rank] + flipped[rank:]
        scatter(round_index, 2, jnp.concatenate([flipped, flipped], axis=0).T)

        receive(round_index, 2)
        send_gram(round_index, 2)
        mixed_c = mix(blk_c[...])
        weights = jnp.concatenate([mixed_c, mixed_c], axis=0)
        sum_b[...] = jnp.zeros_like(sum_b)

        def contract_ab(c, carry):
            rows = pl.ds(pl.multiple_of(c * (CHUNK * n_j), CHUNK * n_j), CHUNK * n_j)
            part_a = pl.ds(pl.multiple_of(c * CHUNK, CHUNK), CHUNK)
            rows_a = blk_a[part_a, :]
            along = jnp.dot(pair_ref[rows, :], weights, preferred_element_type=jnp.float32)
            along = along.reshape(CHUNK, n_j, wide)
            sum_a[part_a, :] = jnp.sum(along * block_b[None], axis=1)
            sum_b[...] += jnp.sum(along * rows_a[:, None, :], axis=0)
            return carry

        lax.fori_loop(0, n_i // CHUNK, contract_ab, 0, unroll=4)
        moment_a, moment_b = sum_a[...], sum_b[...]
        scatter(round_index, 0, moment_a + pltpu.roll(moment_a, rank, 1))
        scatter(round_index, 1, moment_b + pltpu.roll(moment_b, rank, 1))

        totals = []
        for (peers, me, which), gram in zip(lines, grams):
            all_of(gram.at[round_index], peers, 9 * round_index + 3 + which).wait_recv()
            totals.append(sum(gram[round_index, p] for p in range(len(peers) + 1)))
        slopes = [None] * 3
        heads = []
        for which, (p, q) in enumerate(((1, 2), (0, 2), (0, 1))):
            product = mix(jnp.concatenate(unpack(totals[p] * totals[q], rank), axis=0))
            head = jnp.dot(
                mix(own[which]),
                jnp.concatenate([product, product], axis=0),
                preferred_element_type=jnp.float32,
            )
            heads.append(head + pltpu.roll(head, rank, 1))
        for which in (2, 0, 1):
            peers = groups[which][0]
            pull, rows = pulls[which], owned[which].shape[0]
            all_of(pull.at[round_index], peers, 9 * round_index + 6 + which).wait_recv()
            moment = sum(pull[round_index, p] for p in range(len(peers) + 1))
            moment = jnp.concatenate(unpack(moment, rows), axis=0)
            slopes[which] = (heads[which] - moment) / counts[which]
            if round_index + 1 < STEPS:
                own[which] = own[which] - step_size * slopes[which]
                gather(round_index + 1, which, own[which])

    for ref, slope in zip((out_a_ref, out_b_ref, out_c_ref), slopes):
        ref[...] = slope[:, :rank]
    for buffer, peers, slot in finals:
        all_of(buffer, peers, slot).wait_send()


def store(from_a, from_b, from_c, to_a, to_b, to_c, sem):
    copies = [
        pltpu.make_async_copy(source, target, sem.at[p])
        for p, (source, target) in enumerate(((from_a, to_a), (from_b, to_b), (from_c, to_c)))
    ]
    for copy in copies:
        copy.start()
    for copy in copies:
        copy.wait()


def shards(sizes, tensor, factor_a, factor_b, factor_c):
    nx, ny, nz = sizes
    n_i, n_j, n_k = tensor.shape
    rank = factor_a.shape[1]
    wide = 2 * rank
    all_i, all_j, all_k = float(n_i * nx), float(n_j * ny), float(n_k * nz)
    counts = (all_j * all_k, all_i * all_k, all_i * all_j)
    f32 = jnp.float32
    rows = [x.shape[0] for x in (factor_a, factor_b, factor_c)]
    sides = [ny * nz, nx * nz, nx * ny]
    slots = [pltpu.VMEM((STEPS, n, packed_rows(r), wide), f32) for n, r in zip(sides, rows)]
    blocks = [pltpu.VMEM((n, wide), f32) for n in (n_i, n_j, n_k)]
    operands = [
        pltpu.with_memory_space_constraint(x, pltpu.HBM)
        for x in (tensor, factor_a, factor_b, factor_c)
    ]
    slopes = pl.pallas_call(
        functools.partial(kernel, sizes, counts),
        out_shape=[jax.ShapeDtypeStruct(x.shape, f32) for x in (factor_a, factor_b, factor_c)],
        in_specs=[pl.BlockSpec(memory_space=pltpu.HBM)] * 4,
        out_specs=[pl.BlockSpec(memory_space=pltpu.VMEM)] * 3,
        scratch_shapes=[
            *[pltpu.VMEM(x.shape, f32) for x in (factor_a, factor_b, factor_c)],
            pltpu.VMEM(tensor.shape, f32),
            pltpu.VMEM((n_i * n_j, 2 * n_k), jnp.bfloat16),
            *slots,
            *blocks,
            pltpu.VMEM((n_i, wide), f32),
            pltpu.VMEM((n_j, wide), f32),
            pltpu.VMEM((wide, 2 * n_k), f32),
            *slots,
            *slots,
            *[pltpu.VMEM((STEPS, n, rank // 2, wide), f32) for n in sizes],
            pltpu.SemaphoreType.DMA((3,)),
            pltpu.SemaphoreType.DMA((4,)),
            pltpu.SemaphoreType.DMA((9 * STEPS,)),
            pltpu.SemaphoreType.DMA((9 * STEPS,)),
        ],
        compiler_params=pltpu.CompilerParams(
            collective_id=0, has_side_effects=True, vmem_limit_bytes=48 * 1024 * 1024
        ),
    )(*operands)
    return pl.pallas_call(
        store,
        out_shape=[jax.ShapeDtypeStruct(x.shape, f32) for x in (factor_a, factor_b, factor_c)],
        in_specs=[pl.BlockSpec(memory_space=pl.ANY)] * 3,
        out_specs=[pl.BlockSpec(memory_space=pltpu.HBM)] * 3,
        scratch_shapes=[pltpu.SemaphoreType.DMA((3,))],
        compiler_params=pltpu.CompilerParams(vmem_limit_bytes=48 * 1024 * 1024),
    )(*slopes)


def solution(mesh):
    sizes = tuple(mesh.shape[name] for name in ("gx", "gy", "gz"))
    rows = (
        P(("gx", "gy", "gz"), None),
        P(("gy", "gx", "gz"), None),
        P(("gz", "gx", "gy"), None),
    )
    return jax.shard_map(
        functools.partial(shards, sizes),
        mesh=mesh,
        in_specs=(P("gx", "gy", "gz"), *rows),
        out_specs=rows,
        check_vma=False,
    )
```

```python
import functools

import jax
import jax.numpy as jnp
from jax import lax
from jax.experimental import pallas as pl
from jax.experimental.pallas import tpu as pltpu
from jax.sharding import PartitionSpec as P

STEPS = 2
step_size = 0.1
MESH = pl.DeviceIdType.MESH
CHUNK = 8
CHUNK_C = 16
PARTS = 4


def twice(x):
    return jnp.concatenate([x, x], axis=1)


def left_half(shape):
    return lax.broadcasted_iota(jnp.int32, shape, 1) < shape[1] // 2


def packed_rows(rows):
    return rows // 2 if rows % 2 == 0 else rows


def pack(x):
    rows = x.shape[0]
    if rows % 2:
        return x
    return jnp.where(left_half((rows // 2, x.shape[1])), x[: rows // 2], x[rows // 2 :])


def unpack(x, rows):
    if rows % 2:
        return (x,)
    turned = pltpu.roll(x, x.shape[1] // 2, 1)
    left = left_half(x.shape)
    return (jnp.where(left, x, turned), jnp.where(left, turned, x))


def split(x):
    high = x.astype(jnp.bfloat16).astype(jnp.float32)
    return high, x - high


def mix(x):
    high, low = split(x)
    return jnp.where(left_half(x.shape), high, low).astype(jnp.bfloat16)


def kernel(
    sizes,
    counts,
    tensor_hbm,
    own_a_hbm,
    own_b_hbm,
    own_c_hbm,
    out_a_ref,
    out_b_ref,
    out_c_ref,
    own_a_ref,
    own_b_ref,
    own_c_ref,
    tensor_ref,
    pair_ref,
    gat_a,
    gat_b,
    gat_c,
    blk_a,
    blk_b,
    blk_c,
    sum_a,
    sum_b,
    sum_c,
    push_a,
    push_b,
    push_c,
    pull_a,
    pull_b,
    pull_c,
    gram_a,
    gram_b,
    gram_c,
    own_sem,
    load_sem,
    send_sem,
    recv_sem,
):
    nx, ny, nz = sizes
    gx, gy, gz = (lax.axis_index(name) for name in ("gx", "gy", "gz"))
    rank = own_a_ref.shape[1]
    wide = 2 * rank
    n_i, n_j, n_k = tensor_ref.shape

    owned = (own_a_ref, own_b_ref, own_c_ref)
    own_loads = [
        pltpu.make_async_copy(hbm, ref, own_sem.at[p])
        for p, (hbm, ref) in enumerate(zip((own_a_hbm, own_b_hbm, own_c_hbm), owned))
    ]
    for load in own_loads:
        load.start()

    pieces = load_sem.shape[0]
    piece = n_i // pieces
    loads = [
        pltpu.make_async_copy(
            tensor_hbm.at[pl.ds(p * piece, piece)],
            tensor_ref.at[pl.ds(p * piece, piece)],
            load_sem.at[p],
        )
        for p in range(pieces)
    ]
    for load in loads:
        load.start()

    xs = [lax.rem(gx + d, nx) for d in range(nx)]
    ys = [lax.rem(gy + d, ny) for d in range(ny)]
    zs = [lax.rem(gz + d, nz) for d in range(nz)]

    def at(dx, dy, dz):
        return {"gx": xs[dx], "gy": ys[dy], "gz": zs[dz]}

    greeted = [
        (dx, dy, dz)
        for dx in range(nx)
        for dy in range(ny)
        for dz in range(nz)
        if 0 in (dx, dy, dz) and (dx or dy or dz)
    ]
    barrier = pltpu.get_barrier_semaphore()
    for offset in greeted:
        pl.semaphore_signal(barrier, inc=1, device_id=at(*offset), device_id_type=MESH)

    peers_a = [
        (at(0, dy, dz), ys[dy] * nz + zs[dz]) for dy in range(ny) for dz in range(nz) if dy or dz
    ]
    peers_b = [
        (at(dx, 0, dz), xs[dx] * nz + zs[dz]) for dx in range(nx) for dz in range(nz) if dx or dz
    ]
    peers_c = [
        (at(dx, dy, 0), xs[dx] * ny + ys[dy]) for dx in range(nx) for dy in range(ny) if dx or dy
    ]
    groups = (
        (peers_a, gy * nz + gz, 0),
        (peers_b, gx * nz + gz, 1),
        (peers_c, gx * ny + gy, 2),
    )
    lines = (
        ([(at(d, 0, 0), xs[d]) for d in range(1, nx)], gx, 0),
        ([(at(0, d, 0), ys[d]) for d in range(1, ny)], gy, 1),
        ([(at(0, 0, d), zs[d]) for d in range(1, nz)], gz, 2),
    )

    def transfer(src, dst, slot, device):
        return pltpu.make_async_remote_copy(
            src_ref=src,
            dst_ref=dst,
            send_sem=send_sem.at[slot],
            recv_sem=recv_sem.at[slot],
            device_id=device,
            device_id_type=MESH,
        )

    def all_of(buffer, peers, slot):
        some = buffer.at[pl.ds(0, len(peers))]
        return transfer(some, some, slot, peers[0][0])

    finals = []

    gathers = (gat_a, gat_b, gat_c)

    def gather(round_index, which, value):
        peers, me, _ = groups[which]
        buffer, slot = gathers[which], 9 * round_index + which
        buffer[round_index, me] = pack(value)
        for device, _ in peers:
            mine = buffer.at[round_index, me]
            transfer(mine, mine, slot, device).start()
        finals.append((buffer.at[round_index], peers, slot))

    for load in own_loads:
        load.wait()
    own = [twice(ref[...]) for ref in owned]
    pl.semaphore_wait(barrier, len(greeted))
    for which in (1, 0, 2):
        gather(0, which, own[which])

    for p, load in enumerate(loads):
        load.wait()

        def prepare(c, carry):
            block = tensor_ref[pl.ds(c * CHUNK, CHUNK)].reshape(CHUNK * n_j, n_k)
            high, low = split(block)
            rows = pl.ds(pl.multiple_of(c * (CHUNK * n_j), CHUNK * n_j), CHUNK * n_j)
            pair_ref[rows, pl.ds(0, n_k)] = high.astype(jnp.bfloat16)
            pair_ref[rows, pl.ds(n_k, n_k)] = low.astype(jnp.bfloat16)
            return carry

        lax.fori_loop(p * piece // CHUNK, (p + 1) * piece // CHUNK, prepare, 0)

    blocks = (blk_a, blk_b, blk_c)
    grams = (gram_a, gram_b, gram_c)
    pushes, pulls = (push_a, push_b, push_c), (pull_a, pull_b, pull_c)
    half = rank // 2

    def receive(round_index, which):
        peers, me, _ = groups[which]
        buffer, block = gathers[which], blocks[which]
        all_of(buffer.at[round_index], peers, 9 * round_index + which).wait_recv()
        rows = owned[which].shape[0]
        for p in range(len(peers) + 1):
            parts = unpack(buffer[round_index, p], rows)
            step = rows // len(parts)
            for q, part in enumerate(parts):
                block[p * rows + q * step : p * rows + (q + 1) * step] = part

    def send_gram(round_index, which):
        peers, me, _ = lines[which]
        gram, slot = grams[which], 9 * round_index + 3 + which
        mixed = mix(blocks[which][...])
        full = lax.dot_general(
            mixed, mixed, (((0,), (0,)), ((), ())), preferred_element_type=jnp.float32
        )
        full = full[:rank] + full[rank:]
        full = full + pltpu.roll(full, rank, 1)
        gram[round_index, me] = pack(full)
        for device, _ in peers:
            mine = gram.at[round_index, me]
            transfer(mine, mine, slot, device).start()
        finals.append((gram.at[round_index], peers, slot))

    def scatter(round_index, which, moment):
        peers, me, _ = groups[which]
        push, pull, slot = pushes[which], pulls[which], 9 * round_index + 6 + which
        rows = owned[which].shape[0]
        for p in range(len(peers) + 1):
            push[round_index, p] = pack(moment[p * rows : (p + 1) * rows])
        for device, place in peers:
            transfer(push.at[round_index, place], pull.at[round_index, me], slot, device).start()
        pull[round_index, me] = push[round_index, me]
        finals.append((pull.at[round_index], peers, slot))

    def scatter_a(round_index, part):
        me, rows = groups[0][1], own_a_ref.shape[0]
        places = ny * nz // PARTS
        for p in range(part * places, (part + 1) * places):
            moment = sum_a[p * rows : (p + 1) * rows]
            push_a[round_index, p] = pack(moment + pltpu.roll(moment, rank, 1))

            @pl.when(me != p)
            def _():
                device = {"gx": gx, "gy": jnp.int32(p // nz), "gz": jnp.int32(p % nz)}
                transfer(
                    push_a.at[round_index, p],
                    pull_a.at[round_index, me],
                    9 * round_index + 6,
                    device,
                ).start()

    for round_index in range(STEPS):
        receive(round_index, 0)
        receive(round_index, 1)
        send_gram(round_index, 0)
        send_gram(round_index, 1)
        block_b = blk_b[...]

        sum_c[...] = jnp.zeros_like(sum_c)

        def contract_c(c, carry):
            rows = pl.ds(pl.multiple_of(c * (CHUNK_C * n_j), CHUNK_C * n_j), CHUNK_C * n_j)
            rows_a = blk_a[pl.ds(pl.multiple_of(c * CHUNK_C, CHUNK_C), CHUNK_C), :]
            paired = (rows_a[:, None, :] * block_b[None]).reshape(CHUNK_C * n_j, wide)
            mixed = mix(paired)
            sum_c[...] += lax.dot_general(
                mixed,
                pair_ref[rows, :],
                (((0,), (0,)), ((), ())),
                preferred_element_type=jnp.float32,
            )
            return carry

        lax.fori_loop(0, n_i // CHUNK_C, contract_c, 0, unroll=2)
        flipped = sum_c[...]
        flipped = flipped[:, :n_k] + flipped[:, n_k:]
        flipped = flipped[:rank] + flipped[rank:]
        scatter(round_index, 2, jnp.concatenate([flipped, flipped], axis=0).T)

        receive(round_index, 2)
        send_gram(round_index, 2)
        mixed_c = mix(blk_c[...])
        weights = jnp.concatenate([mixed_c, mixed_c], axis=0)
        sum_b[...] = jnp.zeros_like(sum_b)

        def contract_ab(c, carry):
            rows = pl.ds(pl.multiple_of(c * (CHUNK * n_j), CHUNK * n_j), CHUNK * n_j)
            part_a = pl.ds(pl.multiple_of(c * CHUNK, CHUNK), CHUNK)
            rows_a = blk_a[part_a, :]
            along = jnp.dot(pair_ref[rows, :], weights, preferred_element_type=jnp.float32)
            along = along.reshape(CHUNK, n_j, wide)
            sum_a[part_a, :] = jnp.sum(along * block_b[None], axis=1)
            sum_b[...] += jnp.sum(along * rows_a[:, None, :], axis=0)
            return carry

        steps = n_i // CHUNK // PARTS
        for part in range(PARTS):
            lax.fori_loop(part * steps, (part + 1) * steps, contract_ab, 0, unroll=4)
            if part == PARTS - 1:
                moment_b = sum_b[...]
                scatter(round_index, 1, moment_b + pltpu.roll(moment_b, rank, 1))
            scatter_a(round_index, part)
        pull_a[round_index, groups[0][1]] = push_a[round_index, groups[0][1]]
        finals.append((pull_a.at[round_index], peers_a, 9 * round_index + 6))

        totals = []
        for (peers, me, which), gram in zip(lines, grams):
            all_of(gram.at[round_index], peers, 9 * round_index + 3 + which).wait_recv()
            totals.append(sum(gram[round_index, p] for p in range(len(peers) + 1)))
        slopes = [None] * 3
        heads = []
        for which, (p, q) in enumerate(((1, 2), (0, 2), (0, 1))):
            product = mix(jnp.concatenate(unpack(totals[p] * totals[q], rank), axis=0))
            head = jnp.dot(
                mix(own[which]),
                jnp.concatenate([product, product], axis=0),
                preferred_element_type=jnp.float32,
            )
            heads.append(head + pltpu.roll(head, rank, 1))
        for which in (2, 0, 1):
            peers = groups[which][0]
            pull, rows = pulls[which], owned[which].shape[0]
            all_of(pull.at[round_index], peers, 9 * round_index + 6 + which).wait_recv()
            moment = sum(pull[round_index, p] for p in range(len(peers) + 1))
            moment = jnp.concatenate(unpack(moment, rows), axis=0)
            slopes[which] = (heads[which] - moment) / counts[which]
            if round_index + 1 < STEPS:
                own[which] = own[which] - step_size * slopes[which]
                gather(round_index + 1, which, own[which])

    for ref, slope in zip((out_a_ref, out_b_ref, out_c_ref), slopes):
        ref[...] = slope[:, :rank]
    for buffer, peers, slot in finals:
        all_of(buffer, peers, slot).wait_send()


def store(from_a, from_b, from_c, to_a, to_b, to_c, sem):
    copies = [
        pltpu.make_async_copy(source, target, sem.at[p])
        for p, (source, target) in enumerate(((from_a, to_a), (from_b, to_b), (from_c, to_c)))
    ]
    for copy in copies:
        copy.start()
    for copy in copies:
        copy.wait()


def shards(sizes, tensor, factor_a, factor_b, factor_c):
    nx, ny, nz = sizes
    n_i, n_j, n_k = tensor.shape
    rank = factor_a.shape[1]
    wide = 2 * rank
    all_i, all_j, all_k = float(n_i * nx), float(n_j * ny), float(n_k * nz)
    counts = (all_j * all_k, all_i * all_k, all_i * all_j)
    f32 = jnp.float32
    rows = [x.shape[0] for x in (factor_a, factor_b, factor_c)]
    sides = [ny * nz, nx * nz, nx * ny]
    slots = [pltpu.VMEM((STEPS, n, packed_rows(r), wide), f32) for n, r in zip(sides, rows)]
    blocks = [pltpu.VMEM((n, wide), f32) for n in (n_i, n_j, n_k)]
    operands = [
        pltpu.with_memory_space_constraint(x, pltpu.HBM)
        for x in (tensor, factor_a, factor_b, factor_c)
    ]
    slopes = pl.pallas_call(
        functools.partial(kernel, sizes, counts),
        out_shape=[jax.ShapeDtypeStruct(x.shape, f32) for x in (factor_a, factor_b, factor_c)],
        in_specs=[pl.BlockSpec(memory_space=pltpu.HBM)] * 4,
        out_specs=[pl.BlockSpec(memory_space=pltpu.VMEM)] * 3,
        scratch_shapes=[
            *[pltpu.VMEM(x.shape, f32) for x in (factor_a, factor_b, factor_c)],
            pltpu.VMEM(tensor.shape, f32),
            pltpu.VMEM((n_i * n_j, 2 * n_k), jnp.bfloat16),
            *slots,
            *blocks,
            pltpu.VMEM((n_i, wide), f32),
            pltpu.VMEM((n_j, wide), f32),
            pltpu.VMEM((wide, 2 * n_k), f32),
            *slots,
            *slots,
            *[pltpu.VMEM((STEPS, n, rank // 2, wide), f32) for n in sizes],
            pltpu.SemaphoreType.DMA((3,)),
            pltpu.SemaphoreType.DMA((4,)),
            pltpu.SemaphoreType.DMA((9 * STEPS,)),
            pltpu.SemaphoreType.DMA((9 * STEPS,)),
        ],
        compiler_params=pltpu.CompilerParams(
            collective_id=0, has_side_effects=True, vmem_limit_bytes=48 * 1024 * 1024
        ),
    )(*operands)
    return pl.pallas_call(
        store,
        out_shape=[jax.ShapeDtypeStruct(x.shape, f32) for x in (factor_a, factor_b, factor_c)],
        in_specs=[pl.BlockSpec(memory_space=pl.ANY)] * 3,
        out_specs=[pl.BlockSpec(memory_space=pltpu.HBM)] * 3,
        scratch_shapes=[pltpu.SemaphoreType.DMA((3,))],
        compiler_params=pltpu.CompilerParams(vmem_limit_bytes=48 * 1024 * 1024),
    )(*slopes)


def solution(mesh):
    sizes = tuple(mesh.shape[name] for name in ("gx", "gy", "gz"))
    rows = (
        P(("gx", "gy", "gz"), None),
        P(("gy", "gx", "gz"), None),
        P(("gz", "gx", "gy"), None),
    )
    return jax.shard_map(
        functools.partial(shards, sizes),
        mesh=mesh,
        in_specs=(P("gx", "gy", "gz"), *rows),
        out_specs=rows,
        check_vma=False,
    )
```

```python
import functools

import jax
import jax.numpy as jnp
from jax import lax
from jax.experimental import pallas as pl
from jax.experimental.pallas import tpu as pltpu
from jax.sharding import PartitionSpec as P

STEPS = 2
step_size = 0.1
MESH = pl.DeviceIdType.MESH
CHUNK = 8
CHUNK_C = 16


def twice(x):
    return jnp.concatenate([x, x], axis=1)


def left_half(shape):
    return lax.broadcasted_iota(jnp.int32, shape, 1) < shape[1] // 2


def packed_rows(rows):
    return rows // 2 if rows % 2 == 0 else rows


def pack(x):
    rows = x.shape[0]
    if rows % 2:
        return x
    return jnp.where(left_half((rows // 2, x.shape[1])), x[: rows // 2], x[rows // 2 :])


def unpack(x, rows):
    if rows % 2:
        return (x,)
    turned = pltpu.roll(x, x.shape[1] // 2, 1)
    left = left_half(x.shape)
    return (jnp.where(left, x, turned), jnp.where(left, turned, x))


def split(x):
    high = x.astype(jnp.bfloat16).astype(jnp.float32)
    return high, x - high


def mix(x):
    high, low = split(x)
    return jnp.where(left_half(x.shape), high, low).astype(jnp.bfloat16)


def kernel(
    sizes,
    counts,
    tensor_hbm,
    own_a_hbm,
    own_b_hbm,
    own_c_hbm,
    out_a_ref,
    out_b_ref,
    out_c_ref,
    own_a_ref,
    own_b_ref,
    own_c_ref,
    tensor_ref,
    pair_ref,
    gat_a,
    gat_b,
    gat_c,
    blk_a,
    blk_b,
    blk_c,
    sum_a,
    sum_b,
    sum_c,
    push_a,
    push_b,
    push_c,
    pull_a,
    pull_b,
    pull_c,
    gram_a,
    gram_b,
    gram_c,
    own_sem,
    load_sem,
    send_sem,
    recv_sem,
):
    nx, ny, nz = sizes
    gx, gy, gz = (lax.axis_index(name) for name in ("gx", "gy", "gz"))
    rank = own_a_ref.shape[1]
    wide = 2 * rank
    n_i, n_j, n_k = tensor_ref.shape

    owned = (own_a_ref, own_b_ref, own_c_ref)
    own_loads = [
        pltpu.make_async_copy(hbm, ref, own_sem.at[p])
        for p, (hbm, ref) in enumerate(zip((own_a_hbm, own_b_hbm, own_c_hbm), owned))
    ]
    for load in own_loads:
        load.start()

    pieces = load_sem.shape[0]
    piece = n_i // pieces
    loads = [
        pltpu.make_async_copy(
            tensor_hbm.at[pl.ds(p * piece, piece)],
            tensor_ref.at[pl.ds(p * piece, piece)],
            load_sem.at[p],
        )
        for p in range(pieces)
    ]
    for load in loads:
        load.start()

    xs = [lax.rem(gx + d, nx) for d in range(nx)]
    ys = [lax.rem(gy + d, ny) for d in range(ny)]
    zs = [lax.rem(gz + d, nz) for d in range(nz)]

    def at(dx, dy, dz):
        return {"gx": xs[dx], "gy": ys[dy], "gz": zs[dz]}

    greeted = [
        (dx, dy, dz)
        for dx in range(nx)
        for dy in range(ny)
        for dz in range(nz)
        if 0 in (dx, dy, dz) and (dx or dy or dz)
    ]
    barrier = pltpu.get_barrier_semaphore()
    for offset in greeted:
        pl.semaphore_signal(barrier, inc=1, device_id=at(*offset), device_id_type=MESH)

    peers_a = [
        (at(0, dy, dz), ys[dy] * nz + zs[dz]) for dy in range(ny) for dz in range(nz) if dy or dz
    ]
    peers_b = [
        (at(dx, 0, dz), xs[dx] * nz + zs[dz]) for dx in range(nx) for dz in range(nz) if dx or dz
    ]
    peers_c = [
        (at(dx, dy, 0), xs[dx] * ny + ys[dy]) for dx in range(nx) for dy in range(ny) if dx or dy
    ]
    groups = (
        (peers_a, gy * nz + gz, 0),
        (peers_b, gx * nz + gz, 1),
        (peers_c, gx * ny + gy, 2),
    )
    lines = (
        ([(at(d, 0, 0), xs[d]) for d in range(1, nx)], gx, 0),
        ([(at(0, d, 0), ys[d]) for d in range(1, ny)], gy, 1),
        ([(at(0, 0, d), zs[d]) for d in range(1, nz)], gz, 2),
    )

    def transfer(src, dst, slot, device):
        return pltpu.make_async_remote_copy(
            src_ref=src,
            dst_ref=dst,
            send_sem=send_sem.at[slot],
            recv_sem=recv_sem.at[slot],
            device_id=device,
            device_id_type=MESH,
        )

    def all_of(buffer, peers, slot):
        some = buffer.at[pl.ds(0, len(peers))]
        return transfer(some, some, slot, peers[0][0])

    finals = []

    gathers = (gat_a, gat_b, gat_c)

    def gather(round_index, which, value):
        peers, me, _ = groups[which]
        buffer, slot = gathers[which], 9 * round_index + which
        buffer[round_index, me] = pack(value)
        for device, _ in peers:
            mine = buffer.at[round_index, me]
            transfer(mine, mine, slot, device).start()
        finals.append((buffer.at[round_index], peers, slot))

    for load in own_loads:
        load.wait()
    own = [twice(ref[...]) for ref in owned]
    pl.semaphore_wait(barrier, len(greeted))
    for which in range(3):
        gather(0, which, own[which])

    for p, load in enumerate(loads):
        load.wait()

        def prepare(c, carry):
            block = tensor_ref[pl.ds(c * CHUNK, CHUNK)].reshape(CHUNK * n_j, n_k)
            high, low = split(block)
            rows = pl.ds(pl.multiple_of(c * (CHUNK * n_j), CHUNK * n_j), CHUNK * n_j)
            pair_ref[rows, pl.ds(0, n_k)] = high.astype(jnp.bfloat16)
            pair_ref[rows, pl.ds(n_k, n_k)] = low.astype(jnp.bfloat16)
            return carry

        lax.fori_loop(p * piece // CHUNK, (p + 1) * piece // CHUNK, prepare, 0)

    blocks = (blk_a, blk_b, blk_c)
    grams = (gram_a, gram_b, gram_c)
    pushes, pulls = (push_a, push_b, push_c), (pull_a, pull_b, pull_c)
    half = rank // 2

    def receive(round_index, which):
        peers, me, _ = groups[which]
        buffer, block = gathers[which], blocks[which]
        all_of(buffer.at[round_index], peers, 9 * round_index + which).wait_recv()
        rows = owned[which].shape[0]
        for p in range(len(peers) + 1):
            parts = unpack(buffer[round_index, p], rows)
            step = rows // len(parts)
            for q, part in enumerate(parts):
                block[p * rows + q * step : p * rows + (q + 1) * step] = part

    def send_gram(round_index, which):
        peers, me, _ = lines[which]
        gram, slot = grams[which], 9 * round_index + 3 + which
        mixed = mix(blocks[which][...])
        full = lax.dot_general(
            mixed, mixed, (((0,), (0,)), ((), ())), preferred_element_type=jnp.float32
        )
        full = full[:rank] + full[rank:]
        full = full + pltpu.roll(full, rank, 1)
        gram[round_index, me] = pack(full)
        for device, _ in peers:
            mine = gram.at[round_index, me]
            transfer(mine, mine, slot, device).start()
        finals.append((gram.at[round_index], peers, slot))

    def scatter(round_index, which, moment):
        peers, me, _ = groups[which]
        push, pull, slot = pushes[which], pulls[which], 9 * round_index + 6 + which
        rows = owned[which].shape[0]
        for p in range(len(peers) + 1):
            push[round_index, p] = pack(moment[p * rows : (p + 1) * rows])
        for device, place in peers:
            transfer(push.at[round_index, place], pull.at[round_index, me], slot, device).start()
        pull[round_index, me] = push[round_index, me]
        finals.append((pull.at[round_index], peers, slot))

    for round_index in range(STEPS):
        receive(round_index, 0)
        receive(round_index, 1)
        send_gram(round_index, 0)
        send_gram(round_index, 1)
        block_b = blk_b[...]

        sum_c[...] = jnp.zeros_like(sum_c)

        def contract_c(c, carry):
            rows = pl.ds(pl.multiple_of(c * (CHUNK_C * n_j), CHUNK_C * n_j), CHUNK_C * n_j)
            rows_a = blk_a[pl.ds(pl.multiple_of(c * CHUNK_C, CHUNK_C), CHUNK_C), :]
            paired = (rows_a[:, None, :] * block_b[None]).reshape(CHUNK_C * n_j, wide)
            mixed = mix(paired)
            sum_c[...] += lax.dot_general(
                mixed,
                pair_ref[rows, :],
                (((0,), (0,)), ((), ())),
                preferred_element_type=jnp.float32,
            )
            return carry

        lax.fori_loop(0, n_i // CHUNK_C, contract_c, 0, unroll=4)
        flipped = sum_c[...]
        flipped = flipped[:, :n_k] + flipped[:, n_k:]
        flipped = flipped[:rank] + flipped[rank:]
        scatter(round_index, 2, jnp.concatenate([flipped, flipped], axis=0).T)

        receive(round_index, 2)
        send_gram(round_index, 2)
        mixed_c = mix(blk_c[...])
        weights = jnp.concatenate([mixed_c, mixed_c], axis=0)
        sum_b[...] = jnp.zeros_like(sum_b)

        def contract_ab(c, carry):
            rows = pl.ds(pl.multiple_of(c * (CHUNK * n_j), CHUNK * n_j), CHUNK * n_j)
            part_a = pl.ds(pl.multiple_of(c * CHUNK, CHUNK), CHUNK)
            rows_a = blk_a[part_a, :]
            along = jnp.dot(pair_ref[rows, :], weights, preferred_element_type=jnp.float32)
            along = along.reshape(CHUNK, n_j, wide)
            sum_a[part_a, :] = jnp.sum(along * block_b[None], axis=1)
            sum_b[...] += jnp.sum(along * rows_a[:, None, :], axis=0)
            return carry

        lax.fori_loop(0, n_i // CHUNK, contract_ab, 0, unroll=8)
        moment_a, moment_b = sum_a[...], sum_b[...]
        scatter(round_index, 0, moment_a + pltpu.roll(moment_a, rank, 1))
        scatter(round_index, 1, moment_b + pltpu.roll(moment_b, rank, 1))

        totals = []
        for (peers, me, which), gram in zip(lines, grams):
            all_of(gram.at[round_index], peers, 9 * round_index + 3 + which).wait_recv()
            totals.append(sum(gram[round_index, p] for p in range(len(peers) + 1)))
        slopes = [None] * 3
        heads = []
        for which, (p, q) in enumerate(((1, 2), (0, 2), (0, 1))):
            product = mix(jnp.concatenate(unpack(totals[p] * totals[q], rank), axis=0))
            head = jnp.dot(
                mix(own[which]),
                jnp.concatenate([product, product], axis=0),
                preferred_element_type=jnp.float32,
            )
            heads.append(head + pltpu.roll(head, rank, 1))
        for which in (2, 0, 1):
            peers = groups[which][0]
            pull, rows = pulls[which], owned[which].shape[0]
            all_of(pull.at[round_index], peers, 9 * round_index + 6 + which).wait_recv()
            moment = sum(pull[round_index, p] for p in range(len(peers) + 1))
            moment = jnp.concatenate(unpack(moment, rows), axis=0)
            slopes[which] = (heads[which] - moment) / counts[which]
            if round_index + 1 < STEPS:
                own[which] = own[which] - step_size * slopes[which]
                gather(round_index + 1, which, own[which])

    for ref, slope in zip((out_a_ref, out_b_ref, out_c_ref), slopes):
        ref[...] = slope[:, :rank]
    for buffer, peers, slot in finals:
        all_of(buffer, peers, slot).wait_send()


def store(from_a, from_b, from_c, to_a, to_b, to_c, sem):
    copies = [
        pltpu.make_async_copy(source, target, sem.at[p])
        for p, (source, target) in enumerate(((from_a, to_a), (from_b, to_b), (from_c, to_c)))
    ]
    for copy in copies:
        copy.start()
    for copy in copies:
        copy.wait()


def shards(sizes, tensor, factor_a, factor_b, factor_c):
    nx, ny, nz = sizes
    n_i, n_j, n_k = tensor.shape
    rank = factor_a.shape[1]
    wide = 2 * rank
    all_i, all_j, all_k = float(n_i * nx), float(n_j * ny), float(n_k * nz)
    counts = (all_j * all_k, all_i * all_k, all_i * all_j)
    f32 = jnp.float32
    rows = [x.shape[0] for x in (factor_a, factor_b, factor_c)]
    sides = [ny * nz, nx * nz, nx * ny]
    slots = [pltpu.VMEM((STEPS, n, packed_rows(r), wide), f32) for n, r in zip(sides, rows)]
    blocks = [pltpu.VMEM((n, wide), f32) for n in (n_i, n_j, n_k)]
    operands = [
        pltpu.with_memory_space_constraint(x, pltpu.HBM)
        for x in (tensor, factor_a, factor_b, factor_c)
    ]
    slopes = pl.pallas_call(
        functools.partial(kernel, sizes, counts),
        out_shape=[jax.ShapeDtypeStruct(x.shape, f32) for x in (factor_a, factor_b, factor_c)],
        in_specs=[pl.BlockSpec(memory_space=pltpu.HBM)] * 4,
        out_specs=[pl.BlockSpec(memory_space=pltpu.VMEM)] * 3,
        scratch_shapes=[
            *[pltpu.VMEM(x.shape, f32) for x in (factor_a, factor_b, factor_c)],
            pltpu.VMEM(tensor.shape, f32),
            pltpu.VMEM((n_i * n_j, 2 * n_k), jnp.bfloat16),
            *slots,
            *blocks,
            pltpu.VMEM((n_i, wide), f32),
            pltpu.VMEM((n_j, wide), f32),
            pltpu.VMEM((wide, 2 * n_k), f32),
            *slots,
            *slots,
            *[pltpu.VMEM((STEPS, n, rank // 2, wide), f32) for n in sizes],
            pltpu.SemaphoreType.DMA((3,)),
            pltpu.SemaphoreType.DMA((4,)),
            pltpu.SemaphoreType.DMA((9 * STEPS,)),
            pltpu.SemaphoreType.DMA((9 * STEPS,)),
        ],
        compiler_params=pltpu.CompilerParams(
            collective_id=0, has_side_effects=True, vmem_limit_bytes=48 * 1024 * 1024
        ),
    )(*operands)
    return pl.pallas_call(
        store,
        out_shape=[jax.ShapeDtypeStruct(x.shape, f32) for x in (factor_a, factor_b, factor_c)],
        in_specs=[pl.BlockSpec(memory_space=pl.ANY)] * 3,
        out_specs=[pl.BlockSpec(memory_space=pltpu.HBM)] * 3,
        scratch_shapes=[pltpu.SemaphoreType.DMA((3,))],
        compiler_params=pltpu.CompilerParams(vmem_limit_bytes=48 * 1024 * 1024),
    )(*slopes)


def solution(mesh):
    sizes = tuple(mesh.shape[name] for name in ("gx", "gy", "gz"))
    rows = (
        P(("gx", "gy", "gz"), None),
        P(("gy", "gx", "gz"), None),
        P(("gz", "gx", "gy"), None),
    )
    return jax.shard_map(
        functools.partial(shards, sizes),
        mesh=mesh,
        in_specs=(P("gx", "gy", "gz"), *rows),
        out_specs=rows,
        check_vma=False,
    )
```
